256 devices in a mesh: group: 32 (over x_lo, z, core), tensor: 8 (over x_hi, y).
Axes of the slice: x: 4 (x_hi: 2, x_lo: 2; x = x_hi * 2 + x_lo), y: 4, z: 8, core: 2. Of those that a mesh axis runs over, the one named last changes fastest.
Arguments:
- ssm_input: bfloat16 [16384, 16384], P('group', 'tensor'), may hold values from -6 to 6
- gate_input: bfloat16 [16384, 16384], P('group', 'tensor'), may hold values from -12 to 12
- step_sizes: float32 [256, 16384], P('tensor', 'group'), may hold values from 0.25 to 102
- decay_rates: float32 [256], P('tensor'), as said below
- state_write: bfloat16 [16384, 2048], P('group', 'tensor'), may hold values from -0.25 to 0.25
- state_read: bfloat16 [16384, 2048], P('group', 'tensor'), may hold values from -0.375 to 0.375
- norm_gain: float32 [16384], P('tensor'), may hold values from 0.1 to 1.9
- queries: bfloat16 [16384, 8192], P('group', 'tensor'), may hold values from -6 to 6
- suffix_keys: bfloat16 [16384, 1024], P('group', 'tensor'), may hold values from -6 to 6
- suffix_values: bfloat16 [16384, 1024], P('group', 'tensor'), may hold values from -6 to 6
- held_state: bfloat16 [32, 256, 64, 256], P('group', 'tensor'), may hold values from -6 to 6
- held_cache: bfloat16 [32, 2, 512, 1024], P('group', None, None, 'tensor'), may hold values from -6 to 6
- prefix_ids: int32 [32], replicated, may hold values from 0 to 31
- prefix_lengths: int32 [32], replicated, may hold values from 1 to 512, as said below
- holder_slots: int32 [32], replicated, may hold values from 0 to 31, each once
- new_holders: int32 [32], replicated, may hold values from 0 to 31, each once
Outputs:
- ssm_out: bfloat16 [16384, 16384], P('group', 'tensor')
- attn_out: bfloat16 [16384, 8192], P('group', 'tensor')
- stored_state: bfloat16 [32, 256, 64, 256], P('group', 'tensor')
The draws below stay inside these ranges and needn't reach their ends.
Inputs may be any that keep to these rules, and one draw needn't show every extreme that they name: `prefix_lengths`: some prefix has exactly 512 tokens. `holder_slots`: each prefix lives in its own slot. `new_holders`: each slot keeps the state of exactly one request. `decay_rates`: Positive.
All inputs are finite; a program needn't handle non-finite values.
Results may differ from the reference program's by a relative error of at most 0.005.
Values may be sent and summed in bfloat16 or wider, within the bound.
A program may use at most 256 MiB of HBM per device.

```python
import math
import jax
import jax.numpy as jnp
import numpy as np
from jax import lax

MHEADS = 256
MDIM = 64
STATE = 256
SGROUPS = 8
QHEADS = 64
KVHEADS = 8
HDIM = 128
SUFFIX_TOKENS = 512
LP = 512
BLOCK = 256
CACHE_SLOTS = 32
TOKENS = 16384


def draw_queries(key, part):
    key = jax.random.fold_in(key, 3)
    values = jnp.clip(jax.random.normal(key, (TOKENS, QHEADS * HDIM), jnp.float32), -6.0, 6.0)
    return values.astype(jnp.bfloat16)


def draw_suffix_keys(key, part):
    key = jax.random.fold_in(key, 5)
    values = jnp.clip(jax.random.normal(key, (TOKENS, KVHEADS * HDIM), jnp.float32), -6.0, 6.0)
    return values.astype(jnp.bfloat16)


def draw_step_sizes(key, part):
    key = jax.random.fold_in(key, 7)
    first_key, other_key = jax.random.split(key)
    constant_level = jax.random.uniform(first_key, (MHEADS, TOKENS), jnp.float32, 0.5, 1.5)
    spike_events = jax.random.randint(other_key, (CACHE_SLOTS, 2), 0, SUFFIX_TOKENS)
    token_index = jnp.arange(TOKENS)
    holder_index = token_index // SUFFIX_TOKENS
    token_position = token_index % SUFFIX_TOKENS
    spike_mask = (token_position == spike_events[holder_index, 0]) | (token_position == spike_events[holder_index, 1])
    return jnp.where(spike_mask[None, :], SUFFIX_TOKENS // 5 * 1.0, constant_level).astype(jnp.float32)


def draw_decay_rates(key, part):
    key = jax.random.fold_in(key, 9)
    pick_key, slow_key, fast_key = jax.random.split(key, 3)
    cutoff = 4
    slow_heads = jax.random.randint(pick_key, (MHEADS,), 0, 8) < cutoff
    slow_rates = jnp.exp(jax.random.uniform(slow_key, (MHEADS,), jnp.float32, math.log(1.1 / SUFFIX_TOKENS), math.log(1.6 / SUFFIX_TOKENS)))
    fast_rates = jnp.exp(jax.random.uniform(fast_key, (MHEADS,), jnp.float32, math.log(1.0 / 50.0), math.log(1.0 / 30.0)))
    return jnp.where(slow_heads, slow_rates, fast_rates).astype(jnp.float32)


def draw_gate_input(key, part):
    key = jax.random.fold_in(key, 11)
    column = jnp.arange(MHEADS * MDIM) // MDIM
    factor = 1.0 + 2.0 * column / (MHEADS - 1)
    values = jnp.clip(jax.random.normal(key, (TOKENS, MHEADS * MDIM), jnp.float32), -4.0, 4.0) * factor[None, :]
    return values.astype(jnp.bfloat16)


def draw_prefix_lengths(key, part):
    key = jax.random.fold_in(key, 13)
    first_key, other_key = jax.random.split(key)
    lengths = jax.random.randint(first_key, (CACHE_SLOTS,), 1, LP + 1)
    longest = jax.random.randint(other_key, (), 0, CACHE_SLOTS)
    return jnp.where(jnp.arange(CACHE_SLOTS) == longest, LP, lengths).astype(jnp.int32)


def place_ends(result, key, low, top_value):
    shape = result.shape
    index_at = [jax.random.randint(jax.random.fold_in(key, axis), (), 0, shape[axis]) for axis in range(len(shape))]
    result = result.at[tuple(index_at)].set(low)
    longest = shape.index(max(shape))
    index_at[longest] = (index_at[longest] + 1) % shape[longest]
    return result.at[tuple(index_at)].set(top_value)


def shard_levels(key, dims, cuts, smallest, top_value):
    loudness, own = 1.0, jax.random.fold_in(key, 6)
    for dim, blocks in cuts:
        draws = jnp.exp(jax.random.uniform(jax.random.fold_in(own, dim), (blocks,), jnp.float32, smallest / len(cuts), top_value / len(cuts)))
        loudness = loudness * jnp.repeat(draws, dims[dim] // blocks).reshape([-1 if axis == dim else 1 for axis in range(len(dims))])
    return loudness


def rank_table(number_of, slope):
    weights = [(1 << 20) // math.isqrt(standing ** slope) + 1 for standing in range(1, number_of + 1)]
    width = 1 + sum(weights) // (1 << 30)
    return np.cumsum(np.array([max(1, weight // width) for weight in weights]))


def skewed_ids(stream_key, extent, number_of, slope):
    listing = rank_table(number_of, slope)
    pick = jax.random.randint(jax.random.fold_in(stream_key, 1), extent, 0, int(listing[number_of - 1]))
    rank = jnp.searchsorted(jnp.asarray(listing, jnp.int32), pick, side="right")
    return jax.random.permutation(jax.random.fold_in(stream_key, 2), number_of)[rank].astype(jnp.int32)


def normal_values(key, shape, deviation, most, shards=(), kind=jnp.bfloat16):
    result = deviation * jax.random.normal(key, shape, jnp.float32)
    if shards:
        result = result * shard_levels(key, shape, shards, -0.22, 0.18)
    return jnp.clip(result, -most, most).astype(kind)


def setup_inputs(seed: int = 0) -> dict:
    arg_keys = jax.random.split(jax.random.key(seed), 17)
    ssm_input = normal_values(arg_keys[0], (TOKENS, MHEADS * MDIM), 1.0, 6.0, ((0, 32), (1, 8)))
    gate_input = draw_gate_input(jax.random.fold_in(arg_keys[16], 71), 0)
    step_sizes = draw_step_sizes(jax.random.fold_in(arg_keys[16], 71), 0)
    decay_rates = draw_decay_rates(jax.random.fold_in(arg_keys[16], 71), 0)
    state_write = normal_values(arg_keys[4], (TOKENS, SGROUPS * STATE), SUFFIX_TOKENS ** -0.5, 0.25, ((0, 32), (1, 8)))
    state_read = normal_values(arg_keys[5], (TOKENS, SGROUPS * STATE), STATE ** -0.5, 0.375, ((0, 32), (1, 8)))
    norm_gain = jnp.clip(1.0 + 0.18 * jax.random.normal(arg_keys[6], (MHEADS * MDIM,), jnp.float32), 0.1, 1.9)
    queries = draw_queries(jax.random.fold_in(arg_keys[16], 71), 0)
    suffix_keys = draw_suffix_keys(jax.random.fold_in(arg_keys[16], 71), 0)
    suffix_values = normal_values(arg_keys[9], (TOKENS, KVHEADS * HDIM), 1.0, 6.0, ((0, 32), (1, 8)))
    held_state = normal_values(arg_keys[10], (CACHE_SLOTS, MHEADS, MDIM, STATE), 1.0, 6.0, ((0, 32), (1, 8)))
    held_cache = normal_values(arg_keys[11], (CACHE_SLOTS, 2, LP, KVHEADS * HDIM), 1.0, 6.0, ((0, 32), (3, 8)))
    prefix_ids = place_ends(skewed_ids(arg_keys[12], (CACHE_SLOTS,), CACHE_SLOTS, 2), jax.random.fold_in(arg_keys[12], 3), 0, CACHE_SLOTS - 1).astype(jnp.int32)
    prefix_lengths = draw_prefix_lengths(jax.random.fold_in(arg_keys[16], 71), 0)
    holder_slots = jax.random.permutation(arg_keys[14], CACHE_SLOTS).astype(jnp.int32)
    new_holders = jax.random.permutation(arg_keys[15], CACHE_SLOTS).astype(jnp.int32)
    return dict(ssm_input=ssm_input, gate_input=gate_input, step_sizes=step_sizes, decay_rates=decay_rates, state_write=state_write, state_read=state_read, norm_gain=norm_gain, queries=queries, suffix_keys=suffix_keys, suffix_values=suffix_values, held_state=held_state, held_cache=held_cache, prefix_ids=prefix_ids, prefix_lengths=prefix_lengths, holder_slots=holder_slots, new_holders=new_holders)


EPSILON = 1e-05

def scan_head(inputs, size_table, decay_rate, writes, read_table, carried):
    causal_mask = jnp.arange(BLOCK)[:, None] >= jnp.arange(BLOCK)[None, :]
    pieces = []
    for offset in range(0, SUFFIX_TOKENS, BLOCK):
        input_rows = inputs[offset:offset + BLOCK]
        size_rows = size_table[offset:offset + BLOCK]
        write_rows = writes[offset:offset + BLOCK]
        read_rows = read_table[offset:offset + BLOCK]
        cumulative_log = jnp.cumsum(-decay_rate * size_rows)
        log_gaps = jnp.where(causal_mask, cumulative_log[:, None] - cumulative_log[None, :], 0.0)
        decays = jnp.where(causal_mask, jnp.exp(log_gaps), 0.0)
        intersection = jnp.dot(read_rows, write_rows.T, preferred_element_type=jnp.float32)
        weights = (intersection * decays * size_rows[None, :]).astype(jnp.bfloat16)
        ssm_values = jnp.dot(weights, input_rows, preferred_element_type=jnp.float32)
        carried_term = jnp.dot(read_rows.astype(jnp.float32), carried.T, precision=lax.Precision.HIGHEST)
        ssm_values = ssm_values + jnp.exp(cumulative_log)[:, None] * carried_term
        written = (write_rows * (jnp.exp(cumulative_log[-1] - cumulative_log) * size_rows)[:, None]).astype(jnp.bfloat16)
        block_state = jnp.exp(cumulative_log[-1]) * carried + jnp.dot(input_rows.T, written, preferred_element_type=jnp.float32)
        carried = block_state
        pieces.append(ssm_values)
    return (jnp.concatenate(pieces, 0), carried)

def request_ssm(inputs, size_table, head_rates, writes, read_table, start_state, gates, norm_gain):
    per_group = MHEADS // SGROUPS

    def one_head(head_index):
        group_index = head_index // per_group
        head_inputs = lax.dynamic_slice_in_dim(inputs, head_index * MDIM, MDIM, 1)
        head_sizes = lax.dynamic_index_in_dim(size_table, head_index, 0, keepdims=False)
        head_rate = lax.dynamic_index_in_dim(head_rates, head_index, 0, keepdims=False)
        head_writes = lax.dynamic_slice_in_dim(writes, group_index * STATE, STATE, 1)
        head_reads = lax.dynamic_slice_in_dim(read_table, group_index * STATE, STATE, 1)
        head_start = lax.dynamic_index_in_dim(start_state, head_index, 0, keepdims=False).astype(jnp.float32)
        return scan_head(head_inputs, head_sizes, head_rate, head_writes, head_reads, head_start)
    per_head, finals = lax.map(one_head, jnp.arange(MHEADS, dtype=jnp.int32))
    ssm_values = jnp.moveaxis(per_head, 0, 1).reshape(SUFFIX_TOKENS, MHEADS * MDIM)
    final_state = finals.astype(jnp.bfloat16)
    gated_values = ssm_values * jax.nn.silu(gates.astype(jnp.float32))
    mean_square = lax.optimization_barrier(jnp.mean(gated_values * gated_values, axis=1))
    ssm_out = (gated_values * lax.rsqrt(mean_square + EPSILON)[:, None] * norm_gain[None, :]).astype(jnp.bfloat16)
    return (ssm_out, final_state)

def request_attention(query_table, key_table, value_table, cache_rows, length):
    group_share = QHEADS // KVHEADS
    allowed = jnp.concatenate([jnp.broadcast_to(jnp.arange(LP, dtype=jnp.int32)[None, :] < length, (SUFFIX_TOKENS, LP)), jnp.arange(SUFFIX_TOKENS)[None, :] <= jnp.arange(SUFFIX_TOKENS)[:, None]], 1)

    def one_head(head_index):
        kv_index = head_index // group_share
        query_rows = lax.dynamic_slice_in_dim(query_table, head_index * HDIM, HDIM, 1)
        key_all = jnp.concatenate([lax.dynamic_slice_in_dim(cache_rows[0], kv_index * HDIM, HDIM, 1), lax.dynamic_slice_in_dim(key_table, kv_index * HDIM, HDIM, 1)], 0)
        value_all = jnp.concatenate([lax.dynamic_slice_in_dim(cache_rows[1], kv_index * HDIM, HDIM, 1), lax.dynamic_slice_in_dim(value_table, kv_index * HDIM, HDIM, 1)], 0)
        scores = jnp.dot(query_rows, key_all.T, preferred_element_type=jnp.float32) * HDIM ** (-0.5)
        scores = jnp.where(allowed, scores, -jnp.inf)
        highest = lax.optimization_barrier(jnp.max(scores, axis=1, keepdims=True))
        exponents = jnp.exp(scores - highest)
        totals = lax.optimization_barrier(jnp.sum(exponents, axis=1, keepdims=True))
        attention_weights = exponents.astype(jnp.bfloat16)
        return (jnp.dot(attention_weights, value_all, preferred_element_type=jnp.float32) / totals).astype(jnp.bfloat16)
    per_head = lax.map(one_head, jnp.arange(QHEADS, dtype=jnp.int32))
    return jnp.moveaxis(per_head, 0, 1).reshape(SUFFIX_TOKENS, QHEADS * HDIM)

def reference(ssm_input, gate_input, step_sizes, decay_rates, state_write, state_read, norm_gain, queries, suffix_keys, suffix_values, held_state, held_cache, prefix_ids, prefix_lengths, holder_slots, new_holders):
    slot_index = holder_slots[prefix_ids]
    start_state = held_state[slot_index]
    prefix_cache = held_cache[slot_index]
    lengths = prefix_lengths[prefix_ids]

    def one_request(request):
        first_row = request * SUFFIX_TOKENS
        ssm_rows, final_state = request_ssm(lax.dynamic_slice_in_dim(ssm_input, first_row, SUFFIX_TOKENS, 0), lax.dynamic_slice_in_dim(step_sizes, first_row, SUFFIX_TOKENS, 1), decay_rates, lax.dynamic_slice_in_dim(state_write, first_row, SUFFIX_TOKENS, 0), lax.dynamic_slice_in_dim(state_read, first_row, SUFFIX_TOKENS, 0), lax.dynamic_index_in_dim(start_state, request, 0, keepdims=False), lax.dynamic_slice_in_dim(gate_input, first_row, SUFFIX_TOKENS, 0), norm_gain)
        attn_rows = request_attention(lax.dynamic_slice_in_dim(queries, first_row, SUFFIX_TOKENS, 0), lax.dynamic_slice_in_dim(suffix_keys, first_row, SUFFIX_TOKENS, 0), lax.dynamic_slice_in_dim(suffix_values, first_row, SUFFIX_TOKENS, 0), lax.dynamic_index_in_dim(prefix_cache, request, 0, keepdims=False), lax.dynamic_index_in_dim(lengths, request, 0, keepdims=False))
        return (ssm_rows, final_state, attn_rows)
    ssm_rows, finals, attn_rows = lax.map(one_request, jnp.arange(CACHE_SLOTS, dtype=jnp.int32))
    ssm_out = ssm_rows.reshape(TOKENS, MHEADS * MDIM)
    attn_out = attn_rows.reshape(TOKENS, QHEADS * HDIM)
    stored_state = jnp.zeros_like(held_state).at[new_holders].set(finals)
    return (ssm_out, attn_out, stored_state)
```

```python
import jax
import jax.numpy as jnp
from jax import lax
from jax.experimental import pallas as pl
from jax.experimental.pallas import tpu as pltpu
from jax.sharding import PartitionSpec as P

MHEADS = 256
MDIM = 64
STATE = 256
HDIM = 128
BLOCK = 256
ROWS = 512
LP = 512
SLOTS = 32
HEADS = 32
PAIRS = HEADS // 2
QH = 8
RANKS = 8
PIECE = LP // SLOTS
EPSILON = 1e-05
LOW = -1e30
MESH = pl.DeviceIdType.MESH
F32 = jnp.float32
BF16 = jnp.bfloat16


def dot(a, b):
    return jnp.dot(a, b, preferred_element_type=F32)


def dot_nt(a, b):
    return lax.dot_general(a, b, (((1,), (1,)), ((), ())), preferred_element_type=F32)


def kernel(
    ids,
    lengths,
    holders,
    sources,
    rates,
    steps,
    gain,
    x_hbm,
    gate_hbm,
    write_hbm,
    read_hbm,
    q_hbm,
    sk_hbm,
    sv_hbm,
    held,
    cache,
    ssm_out,
    attn_out,
    stored,
    x_v,
    gate_v,
    write_v,
    read_v,
    q_v,
    sk_v,
    sv_v,
    cum_v,
    scale_v,
    fade_v,
    gram_v,
    entry_v,
    y_v,
    decay_v,
    held_a,
    cache_a,
    local_mine,
    local_a,
    total_mine,
    total_a,
    held_p,
    held_b,
    cache_p,
    cache_b,
    final_p,
    attn_v,
    norm_v,
    square_mine,
    square_a,
    in_sem,
    out_sem,
    own_sem,
    send_sem,
    recv_sem,
):
    me = lax.axis_index("group")
    rank = lax.axis_index("tensor")

    loads = []
    for n, (src, dst) in enumerate(
        (
            (x_hbm, x_v),
            (write_hbm, write_v),
            (read_hbm, read_v),
            (q_hbm, q_v),
            (sk_hbm, sk_v),
            (sv_hbm, sv_v),
            (gate_hbm, gate_v),
        )
    ):
        loads.append(pltpu.make_async_copy(src, dst, in_sem.at[n]))
        loads[-1].start()

    barrier = pltpu.get_barrier_semaphore()

    def greet_member(k, carry):
        pl.semaphore_signal(
            barrier, inc=1, device_id={"group": lax.rem(me + k, SLOTS)}, device_id_type=MESH
        )
        return carry

    def greet_rank(k, carry):
        pl.semaphore_signal(
            barrier, inc=1, device_id={"tensor": lax.rem(rank + k, RANKS)}, device_id_type=MESH
        )
        return carry

    lax.fori_loop(1, SLOTS, greet_member, 0)
    lax.fori_loop(1, RANKS, greet_rank, 0)

    def head_logs(h, carry):
        row = pl.ds(h, 1)
        cum_v[row, :] = steps[row, :] * -rates[h]
        return carry

    lax.fori_loop(0, HEADS, head_logs, 0)
    at_u = lax.broadcasted_iota(jnp.int32, (BLOCK, BLOCK), 0)
    at_t = lax.broadcasted_iota(jnp.int32, (BLOCK, BLOCK), 1)
    upper = (at_u <= at_t).astype(F32)
    ends = []
    for b in range(2):
        cols = slice(b * BLOCK, (b + 1) * BLOCK)
        cum = jnp.dot(
            cum_v[:, cols], upper, preferred_element_type=F32, precision=lax.Precision.HIGHEST
        )
        end = cum[:, BLOCK - 1 : BLOCK]
        cum_v[:, cols] = cum
        scale_v[:, cols] = jnp.exp(end - cum) * steps[:, cols]
        ends.append(end)
    fade_v[...] = jnp.broadcast_to(jnp.exp(ends[1]), (HEADS, STATE))
    total_mine[...] = jnp.broadcast_to(jnp.exp(ends[0] + ends[1]), (HEADS, 128)).reshape(
        HEADS, 1, 128
    )

    pl.semaphore_wait(barrier, SLOTS - 1 + RANKS - 1)

    def to_member(p, src, dst, n):
        return pltpu.make_async_remote_copy(
            src_ref=src,
            dst_ref=dst,
            send_sem=send_sem.at[n],
            recv_sem=recv_sem.at[n],
            device_id={"group": p},
            device_id_type=MESH,
        )

    def arrived(buf, n, count=SLOTS - 1):
        part = buf.at[pl.ds(0, count)]
        pltpu.make_async_copy(part, part, recv_sem.at[n]).wait()

    def sent(buf, n, count=SLOTS - 1):
        part = buf.at[pl.ds(0, count)]
        pltpu.make_async_copy(part, part, send_sem.at[n]).wait()

    def cache_rows(p):
        return cache.at[0, :, pl.ds(pl.multiple_of(p * PIECE, PIECE), PIECE), :]

    def spread_cache(k, carry):
        p = lax.rem(me + k, SLOTS)
        to_member(p, cache_rows(p), cache_a.at[me], 0).start()
        return carry

    def spread_held(k, carry):
        p = lax.rem(me + k, SLOTS)
        to_member(p, held.at[0, p], held_a.at[me], 1).start()
        return carry

    lax.fori_loop(1, SLOTS, spread_cache, 0)
    lax.fori_loop(1, SLOTS, spread_held, 0)
    own_cache = pltpu.make_async_copy(cache_rows(me), cache_a.at[me], own_sem.at[0])
    own_held = pltpu.make_async_copy(held.at[0, me], held_a.at[me], own_sem.at[1])
    own_cache.start()
    own_held.start()

    loads[0].wait()
    loads[1].wait()
    first_row = lax.broadcasted_iota(jnp.int32, (2 * MDIM, 1), 0) < MDIM

    def local_state(j, carry):
        a, b = pl.ds(2 * j, 1), pl.ds(2 * j + 1, 1)
        pair = pl.ds(pl.multiple_of(j * 128, 128), 128)
        turned = jnp.transpose(x_v[:, pair].astype(F32))
        scaled = (turned * jnp.where(first_row, scale_v[a, :], scale_v[b, :])).astype(BF16)
        entry = dot(scaled[:, :BLOCK], write_v[:BLOCK, :])
        later = dot(scaled[:, BLOCK:], write_v[BLOCK:, :])
        entry_v[j] = entry.astype(BF16)
        fade = jnp.where(first_row, fade_v[a, :], fade_v[b, :])
        local_mine[pl.ds(2 * j, 2)] = (
            (fade * entry + later).astype(BF16).reshape(2, MDIM, STATE)
        )
        return carry

    lax.fori_loop(0, PAIRS, local_state, 0)

    def spread_local(k, carry):
        p = lax.rem(me + k, SLOTS)
        to_member(p, local_mine.at[p], local_a.at[me], 2).start()
        to_member(p, total_mine.at[p], total_a.at[me], 3).start()
        return carry

    lax.fori_loop(1, SLOTS, spread_local, 0)
    local_a[me] = local_mine[me]
    total_a[me] = total_mine[me]

    own_cache.wait()
    arrived(cache_a, 0)

    def pick_cache(r, carry):
        cache_p[r] = cache_a[holders[ids[r]]]
        return carry

    lax.fori_loop(0, SLOTS, pick_cache, 0)

    def gather_cache(k, carry):
        p = lax.rem(me + k, SLOTS)
        to_member(p, cache_p.at[p], cache_b.at[me], 4).start()
        return carry

    lax.fori_loop(1, SLOTS, gather_cache, 0)
    cache_b[me] = cache_p[me]

    loads[2].wait()
    for b in range(2):
        rows = slice(b * BLOCK, (b + 1) * BLOCK)
        gram_v[b] = dot_nt(read_v[rows, :], write_v[rows, :])
    first_lane = lax.broadcasted_iota(jnp.int32, (1, 128), 1) < MDIM
    causal = at_u >= at_t

    def inner_values(j, carry):
        pair = pl.ds(pl.multiple_of(j * 128, 128), 128)
        xs = x_v[:, pair]
        zero = jnp.zeros_like(xs)
        halves = (jnp.where(first_lane, xs, zero), jnp.where(first_lane, zero, xs))
        tall = []
        values = [None, None]
        for i in range(2):
            row = pl.ds(2 * j + i, 1)
            cum = cum_v[row, :]
            column = jnp.transpose(jnp.broadcast_to(cum, (128, ROWS)))
            tall.append(column)
            for b in range(2):
                rows = slice(b * BLOCK, (b + 1) * BLOCK)
                left = column[rows, :]
                gap = jnp.concatenate([left, left], axis=1) - cum[:, rows]
                decays = jnp.exp(jnp.where(causal, gap, LOW))
                weights = (gram_v[b] * decays * steps[row, rows]).astype(BF16)
                part = dot(weights, halves[i][rows, :])
                values[b] = part if values[b] is None else values[b] + part
        column = jnp.where(first_lane, tall[0], tall[1])
        early, late = column[:BLOCK, :], column[BLOCK:, :]
        entered = dot_nt(read_v[BLOCK:, :], entry_v[j])
        decay_v[j, :BLOCK, :] = jnp.exp(early)
        decay_v[j, BLOCK:, :] = jnp.exp(late + early[BLOCK - 1 : BLOCK, :])
        y_v[j, :BLOCK, :] = values[0]
        y_v[j, BLOCK:, :] = values[1] + jnp.exp(late) * entered
        return carry

    lax.fori_loop(0, PAIRS, inner_values, 0)

    own_held.wait()
    arrived(held_a, 1)

    def pick_held(r, carry):
        held_p[r] = held_a[holders[ids[r]]]
        return carry

    lax.fori_loop(0, SLOTS, pick_held, 0)

    def gather_held(k, carry):
        p = lax.rem(me + k, SLOTS)
        to_member(p, held_p.at[p], held_b.at[me], 5).start()
        return carry

    lax.fori_loop(1, SLOTS, gather_held, 0)
    held_b[me] = held_p[me]

    for n in (3, 4, 5):
        loads[n].wait()
    arrived(cache_b, 4)
    length = lengths[ids[me]]
    prefix_allowed = lax.broadcasted_iota(jnp.int32, (1, LP), 1) < length
    score_scale = HDIM ** (-0.5)

    def attend(h, carry):
        head = pl.ds(pl.multiple_of(h * HDIM, HDIM), HDIM)
        prefix_keys = cache_b[:, 0].reshape(LP, HDIM)
        prefix_values = cache_b[:, 1].reshape(LP, HDIM)
        for b in range(2):
            rows = slice(b * BLOCK, (b + 1) * BLOCK)
            width = (b + 1) * BLOCK
            q = q_v[rows, head]
            prefix = dot_nt(q, prefix_keys) * score_scale
            prefix = jnp.where(prefix_allowed, prefix, LOW)
            own = dot_nt(q, sk_v[:width, :]) * score_scale
            t = lax.broadcasted_iota(jnp.int32, (BLOCK, width), 0) + b * BLOCK
            u = lax.broadcasted_iota(jnp.int32, (BLOCK, width), 1)
            own = jnp.where(u <= t, own, LOW)
            highest = jnp.maximum(
                jnp.max(prefix, axis=1, keepdims=True), jnp.max(own, axis=1, keepdims=True)
            )
            prefix = jnp.exp(prefix - highest)
            own = jnp.exp(own - highest)
            totals = jnp.sum(prefix, axis=1, keepdims=True) + jnp.sum(own, axis=1, keepdims=True)
            mixed = dot(prefix.astype(BF16), prefix_values) + dot(own.astype(BF16), sv_v[:width, :])
            attn_v[rows, head] = (mixed / totals).astype(BF16)
        return carry

    lax.fori_loop(0, QH, attend, 0)
    attn_store = pltpu.make_async_copy(attn_v, attn_out, out_sem.at[0])
    attn_store.start()

    arrived(local_a, 2)
    arrived(total_a, 3)

    def pick_final(d, carry):
        r = sources[d]
        start = held_a[holders[ids[r]]].astype(F32)
        fade = total_a[r]
        fade = jnp.concatenate([fade, fade], axis=1)
        final_p[d] = (start * fade + local_a[r].astype(F32)).astype(BF16)
        return carry

    lax.fori_loop(0, SLOTS, pick_final, 0)

    def store_final(k, carry):
        p = lax.rem(me + k, SLOTS)
        to_member(p, final_p.at[p], stored.at[0, me], 6).start()
        return carry

    lax.fori_loop(1, SLOTS, store_final, 0)
    own_final = pltpu.make_async_copy(final_p.at[me], stored.at[0, me], own_sem.at[2])
    own_final.start()

    loads[6].wait()
    arrived(held_b, 5)

    def gate_values(j, squares):
        pair = pl.ds(pl.multiple_of(j * 128, 128), 128)
        start = held_b[pl.ds(2 * j, 2)].reshape(2 * MDIM, STATE)
        values = y_v[j] + decay_v[j] * dot_nt(read_v[...], start)
        gate = gate_v[:, pair].astype(F32)
        values = values * (gate / (1.0 + jnp.exp(-gate)))
        y_v[j] = values
        return squares + values * values

    squares = lax.fori_loop(0, PAIRS, gate_values, jnp.zeros((ROWS, 128), F32))
    square_mine[...] = jnp.sum(jnp.transpose(squares), axis=0, keepdims=True)

    def send_squares(k, carry):
        pltpu.make_async_remote_copy(
            src_ref=square_mine,
            dst_ref=square_a.at[rank],
            send_sem=send_sem.at[7],
            recv_sem=recv_sem.at[7],
            device_id={"tensor": lax.rem(rank + k, RANKS)},
            device_id_type=MESH,
        ).start()
        return carry

    lax.fori_loop(1, RANKS, send_squares, 0)
    square_a[rank] = square_mine[...]
    arrived(square_a, 7, RANKS - 1)
    mean_square = jnp.sum(square_a[...], axis=0) / (MHEADS * MDIM)
    inverse = lax.rsqrt(mean_square + EPSILON)
    inverse = jnp.transpose(jnp.broadcast_to(inverse, (128, ROWS)))

    def norm(j, carry):
        pair = pl.ds(pl.multiple_of(j * 128, 128), 128)
        norm_v[:, pair] = (y_v[j] * inverse * gain[pl.ds(j, 1), :]).astype(BF16)
        return carry

    lax.fori_loop(0, PAIRS, norm, 0)
    norm_store = pltpu.make_async_copy(norm_v, ssm_out, out_sem.at[1])
    norm_store.start()

    attn_store.wait()
    norm_store.wait()
    own_final.wait()
    sent(cache_a, 0)
    sent(held_a, 1)
    sent(local_a, 2)
    sent(total_a, 3)
    sent(cache_b, 4)
    sent(held_b, 5)
    sent(final_p, 6)
    sent(square_a, 7, RANKS - 1)
    part = stored.at[0, pl.ds(0, SLOTS - 1)]
    pltpu.make_async_copy(part, part, recv_sem.at[6]).wait()


def local(
    ssm_input,
    gate_input,
    step_sizes,
    decay_rates,
    state_write,
    state_read,
    norm_gain,
    queries,
    suffix_keys,
    suffix_values,
    held_state,
    held_cache,
    prefix_ids,
    prefix_lengths,
    holder_slots,
    new_holders,
):
    slots = jnp.arange(SLOTS, dtype=jnp.int32)
    sources = jnp.sum(jnp.where(new_holders[None, :] == slots[:, None], slots[None, :], 0), 1)
    smem = pl.BlockSpec(memory_space=pltpu.SMEM)
    vmem = pl.BlockSpec(memory_space=pltpu.VMEM)
    anywhere = pl.BlockSpec(memory_space=pl.ANY)
    state = (SLOTS, MDIM, STATE)
    cache = (SLOTS, 2, PIECE, HDIM)
    return pl.pallas_call(
        kernel,
        out_shape=(
            jax.ShapeDtypeStruct((ROWS, HEADS * MDIM), BF16),
            jax.ShapeDtypeStruct((ROWS, QH * HDIM), BF16),
            jax.ShapeDtypeStruct((1,) + state, BF16),
        ),
        in_specs=[smem] * 5 + [vmem] * 2 + [anywhere] * 9,
        out_specs=(anywhere,) * 3,
        scratch_shapes=[
            pltpu.VMEM((ROWS, HEADS * MDIM), BF16),
            pltpu.VMEM((ROWS, HEADS * MDIM), BF16),
            pltpu.VMEM((ROWS, STATE), BF16),
            pltpu.VMEM((ROWS, STATE), BF16),
            pltpu.VMEM((ROWS, QH * HDIM), BF16),
            pltpu.VMEM((ROWS, HDIM), BF16),
            pltpu.VMEM((ROWS, HDIM), BF16),
            pltpu.VMEM((HEADS, ROWS), F32),
            pltpu.VMEM((HEADS, ROWS), F32),
            pltpu.VMEM((HEADS, STATE), F32),
            pltpu.VMEM((2, BLOCK, BLOCK), F32),
            pltpu.VMEM((PAIRS, 2 * MDIM, STATE), BF16),
            pltpu.VMEM((PAIRS, ROWS, 128), F32),
            pltpu.VMEM((PAIRS, ROWS, 128), F32),
            pltpu.VMEM(state, BF16),
            pltpu.VMEM(cache, BF16),
            pltpu.VMEM(state, BF16),
            pltpu.VMEM(state, BF16),
            pltpu.VMEM((HEADS, 1, 128), F32),
            pltpu.VMEM((SLOTS, 1, 128), F32),
            pltpu.VMEM(state, BF16),
            pltpu.VMEM(state, BF16),
            pltpu.VMEM(cache, BF16),
            pltpu.VMEM(cache, BF16),
            pltpu.VMEM(state, BF16),
            pltpu.VMEM((ROWS, QH * HDIM), BF16),
            pltpu.VMEM((ROWS, HEADS * MDIM), BF16),
            pltpu.VMEM((1, ROWS), F32),
            pltpu.VMEM((RANKS, 1, ROWS), F32),
            pltpu.SemaphoreType.DMA((7,)),
            pltpu.SemaphoreType.DMA((2,)),
            pltpu.SemaphoreType.DMA((3,)),
            pltpu.SemaphoreType.DMA((8,)),
            pltpu.SemaphoreType.DMA((8,)),
        ],
        compiler_params=pltpu.CompilerParams(
            collective_id=0, has_side_effects=True, vmem_limit_bytes=52 * 2**20
        ),
        name="layer_pair",
    )(
        prefix_ids,
        prefix_lengths,
        holder_slots,
        sources,
        decay_rates,
        step_sizes,
        norm_gain.reshape(PAIRS, 128),
        ssm_input,
        gate_input,
        state_write,
        state_read,
        queries,
        suffix_keys,
        suffix_values,
        held_state,
        held_cache,
    )


def solution(mesh):
    return jax.shard_map(
        local,
        mesh=mesh,
        in_specs=(
            P("group", "tensor"),
            P("group", "tensor"),
            P("tensor", "group"),
            P("tensor"),
            P("group", "tensor"),
            P("group", "tensor"),
            P("tensor"),
            P("group", "tensor"),
            P("group", "tensor"),
            P("group", "tensor"),
            P("group", "tensor", None, None),
            P("group", None, None, "tensor"),
            P(),
            P(),
            P(),
            P(),
        ),
        out_specs=(P("group", "tensor"), P("group", "tensor"), P("group", "tensor", None, None)),
        check_vma=False,
    )
```

```python
import jax
import jax.numpy as jnp
from jax import lax
from jax.experimental import pallas as pl
from jax.experimental.pallas import tpu as pltpu
from jax.sharding import PartitionSpec as P

MHEADS = 256
MDIM = 64
STATE = 256
HDIM = 128
BLOCK = 256
ROWS = 512
LP = 512
SLOTS = 32
HEADS = 32
PAIRS = HEADS // 2
QH = 8
RANKS = 8
PIECE = LP // SLOTS
EPSILON = 1e-05
LOW = -1e30
MESH = pl.DeviceIdType.MESH
F32 = jnp.float32
BF16 = jnp.bfloat16


def dot(a, b):
    return jnp.dot(a, b, preferred_element_type=F32)


def dot_nt(a, b):
    return lax.dot_general(a, b, (((1,), (1,)), ((), ())), preferred_element_type=F32)


def kernel(
    ids_hbm,
    lengths_hbm,
    holders_hbm,
    new_hbm,
    rates_hbm,
    steps_hbm,
    gain_hbm,
    x_hbm,
    gate_hbm,
    write_hbm,
    read_hbm,
    q_hbm,
    sk_hbm,
    sv_hbm,
    held,
    cache,
    ssm_out,
    attn_out,
    stored,
    ids,
    lengths,
    holders,
    new_holders,
    sources,
    rates,
    steps,
    gain,
    x_v,
    gate_v,
    write_v,
    read_v,
    q_v,
    sk_v,
    sv_v,
    cum_v,
    scale_v,
    fade_v,
    gram_v,
    entry_v,
    y_v,
    decay_v,
    held_a,
    cache_a,
    local_mine,
    local_a,
    total_mine,
    total_a,
    held_p,
    held_b,
    cache_p,
    cache_b,
    final_p,
    square_mine,
    square_a,
    in_sem,
    own_sem,
    send_sem,
    recv_sem,
):
    me = lax.axis_index("group")
    rank = lax.axis_index("tensor")

    loads = []
    for n, (src, dst) in enumerate(
        (
            (x_hbm, x_v),
            (write_hbm, write_v),
            (read_hbm, read_v),
            (q_hbm, q_v),
            (sk_hbm, sk_v),
            (sv_hbm, sv_v),
            (gate_hbm, gate_v),
            (rates_hbm, rates),
            (steps_hbm, steps),
            (ids_hbm, ids),
            (lengths_hbm, lengths),
            (holders_hbm, holders),
            (new_hbm, new_holders),
            (gain_hbm, gain),
        )
    ):
        loads.append(pltpu.make_async_copy(src, dst, in_sem.at[n]))
        loads[-1].start()

    barrier = pltpu.get_barrier_semaphore()

    def greet_member(k, carry):
        pl.semaphore_signal(
            barrier, inc=1, device_id={"group": lax.rem(me + k, SLOTS)}, device_id_type=MESH
        )
        return carry

    def greet_rank(k, carry):
        pl.semaphore_signal(
            barrier, inc=1, device_id={"tensor": lax.rem(rank + k, RANKS)}, device_id_type=MESH
        )
        return carry

    lax.fori_loop(1, SLOTS, greet_member, 0)
    lax.fori_loop(1, RANKS, greet_rank, 0)

    loads[7].wait()
    loads[8].wait()

    def head_logs(h, carry):
        row = pl.ds(h, 1)
        cum_v[row, :] = steps[row, :] * -rates[h]
        return carry

    lax.fori_loop(0, HEADS, head_logs, 0)
    at_u = lax.broadcasted_iota(jnp.int32, (BLOCK, BLOCK), 0)
    at_t = lax.broadcasted_iota(jnp.int32, (BLOCK, BLOCK), 1)
    upper = (at_u <= at_t).astype(F32)
    ends = []
    for b in range(2):
        cols = slice(b * BLOCK, (b + 1) * BLOCK)
        cum = jnp.dot(
            cum_v[:, cols], upper, preferred_element_type=F32, precision=lax.Precision.HIGHEST
        )
        end = cum[:, BLOCK - 1 : BLOCK]
        cum_v[:, cols] = cum
        scale_v[:, cols] = jnp.exp(end - cum) * steps[:, cols]
        ends.append(end)
    fade_v[...] = jnp.broadcast_to(jnp.exp(ends[1]), (HEADS, STATE))
    total_mine[...] = jnp.broadcast_to(jnp.exp(ends[0] + ends[1]), (HEADS, 128)).reshape(
        HEADS, 1, 128
    )

    pl.semaphore_wait(barrier, SLOTS - 1 + RANKS - 1)

    def to_member(p, src, dst, n):
        return pltpu.make_async_remote_copy(
            src_ref=src,
            dst_ref=dst,
            send_sem=send_sem.at[n],
            recv_sem=recv_sem.at[n],
            device_id={"group": p},
            device_id_type=MESH,
        )

    def arrived(buf, n, count=SLOTS - 1):
        part = buf.at[pl.ds(0, count)]
        pltpu.make_async_copy(part, part, recv_sem.at[n]).wait()

    def sent(buf, n, count=SLOTS - 1):
        part = buf.at[pl.ds(0, count)]
        pltpu.make_async_copy(part, part, send_sem.at[n]).wait()

    def cache_rows(p):
        return cache.at[0, :, pl.ds(pl.multiple_of(p * PIECE, PIECE), PIECE), :]

    def spread_cache(k, carry):
        p = lax.rem(me + k, SLOTS)
        to_member(p, cache_rows(p), cache_a.at[me], 0).start()
        return carry

    def spread_held(k, carry):
        p = lax.rem(me + k, SLOTS)
        to_member(p, held.at[0, p], held_a.at[me], 1).start()
        return carry

    lax.fori_loop(1, SLOTS, spread_cache, 0)
    lax.fori_loop(1, SLOTS, spread_held, 0)
    own_cache = pltpu.make_async_copy(cache_rows(me), cache_a.at[me], own_sem.at[0])
    own_held = pltpu.make_async_copy(held.at[0, me], held_a.at[me], own_sem.at[1])
    own_cache.start()
    own_held.start()

    for n in range(9, 14):
        loads[n].wait()

    def find_source(d, carry):
        source = 0
        for r in range(1, SLOTS):
            source = jnp.where(new_holders[r] == d, r, source)
        sources[d] = source
        return carry

    lax.fori_loop(0, SLOTS, find_source, 0)

    loads[0].wait()
    loads[1].wait()
    first_row = lax.broadcasted_iota(jnp.int32, (2 * MDIM, 1), 0) < MDIM

    def local_state(j, carry):
        a, b = pl.ds(2 * j, 1), pl.ds(2 * j + 1, 1)
        pair = pl.ds(pl.multiple_of(j * 128, 128), 128)
        turned = jnp.transpose(x_v[:, pair].astype(F32))
        scaled = (turned * jnp.where(first_row, scale_v[a, :], scale_v[b, :])).astype(BF16)
        entry = dot(scaled[:, :BLOCK], write_v[:BLOCK, :])
        later = dot(scaled[:, BLOCK:], write_v[BLOCK:, :])
        entry_v[j] = entry.astype(BF16)
        fade = jnp.where(first_row, fade_v[a, :], fade_v[b, :])
        local_mine[pl.ds(2 * j, 2)] = (
            (fade * entry + later).astype(BF16).reshape(2, MDIM, STATE)
        )
        return carry

    lax.fori_loop(0, PAIRS, local_state, 0)

    def spread_local(k, carry):
        p = lax.rem(me + k, SLOTS)
        to_member(p, local_mine.at[p], local_a.at[me], 2).start()
        to_member(p, total_mine.at[p], total_a.at[me], 3).start()
        return carry

    lax.fori_loop(1, SLOTS, spread_local, 0)
    local_a[me] = local_mine[me]
    total_a[me] = total_mine[me]

    own_cache.wait()
    arrived(cache_a, 0)

    def pick_cache(r, carry):
        cache_p[r] = cache_a[holders[ids[r]]]
        return carry

    lax.fori_loop(0, SLOTS, pick_cache, 0)

    def gather_cache(k, carry):
        p = lax.rem(me + k, SLOTS)
        to_member(p, cache_p.at[p], cache_b.at[me], 4).start()
        return carry

    lax.fori_loop(1, SLOTS, gather_cache, 0)
    cache_b[me] = cache_p[me]

    loads[2].wait()
    for b in range(2):
        rows = slice(b * BLOCK, (b + 1) * BLOCK)
        gram_v[b] = dot_nt(read_v[rows, :], write_v[rows, :])
    first_lane = lax.broadcasted_iota(jnp.int32, (1, 128), 1) < MDIM
    causal = at_u >= at_t

    def inner_values(j, carry):
        pair = pl.ds(pl.multiple_of(j * 128, 128), 128)
        xs = x_v[:, pair]
        zero = jnp.zeros_like(xs)
        halves = (jnp.where(first_lane, xs, zero), jnp.where(first_lane, zero, xs))
        tall = []
        values = [None, None]
        for i in range(2):
            row = pl.ds(2 * j + i, 1)
            cum = cum_v[row, :]
            column = jnp.transpose(jnp.broadcast_to(cum, (128, ROWS)))
            tall.append(column)
            for b in range(2):
                rows = slice(b * BLOCK, (b + 1) * BLOCK)
                left = column[rows, :]
                gap = jnp.concatenate([left, left], axis=1) - cum[:, rows]
                decays = jnp.exp(jnp.where(causal, gap, LOW))
                weights = (gram_v[b] * decays * steps[row, rows]).astype(BF16)
                part = dot(weights, halves[i][rows, :])
                values[b] = part if values[b] is None else values[b] + part
        column = jnp.where(first_lane, tall[0], tall[1])
        early, late = column[:BLOCK, :], column[BLOCK:, :]
        entered = dot_nt(read_v[BLOCK:, :], entry_v[j])
        decay_v[j, :BLOCK, :] = jnp.exp(early)
        decay_v[j, BLOCK:, :] = jnp.exp(late + early[BLOCK - 1 : BLOCK, :])
        y_v[j, :BLOCK, :] = values[0]
        y_v[j, BLOCK:, :] = values[1] + jnp.exp(late) * entered
        return carry

    lax.fori_loop(0, PAIRS, inner_values, 0)

    own_held.wait()
    arrived(held_a, 1)

    def pick_held(r, carry):
        held_p[r] = held_a[holders[ids[r]]]
        return carry

    lax.fori_loop(0, SLOTS, pick_held, 0)

    def gather_held(k, carry):
        p = lax.rem(me + k, SLOTS)
        to_member(p, held_p.at[p], held_b.at[me], 5).start()
        return carry

    lax.fori_loop(1, SLOTS, gather_held, 0)
    held_b[me] = held_p[me]

    for n in (3, 4, 5):
        loads[n].wait()
    arrived(cache_b, 4)
    length = lengths[ids[me]]
    prefix_allowed = lax.broadcasted_iota(jnp.int32, (1, LP), 1) < length
    score_scale = HDIM ** (-0.5)

    def attend(h, carry):
        head = pl.ds(pl.multiple_of(h * HDIM, HDIM), HDIM)
        prefix_keys = cache_b[:, 0].reshape(LP, HDIM)
        prefix_values = cache_b[:, 1].reshape(LP, HDIM)
        for b in range(2):
            rows = slice(b * BLOCK, (b + 1) * BLOCK)
            width = (b + 1) * BLOCK
            q = q_v[rows, head]
            prefix = dot_nt(q, prefix_keys) * score_scale
            prefix = jnp.where(prefix_allowed, prefix, LOW)
            own = dot_nt(q, sk_v[:width, :]) * score_scale
            t = lax.broadcasted_iota(jnp.int32, (BLOCK, width), 0) + b * BLOCK
            u = lax.broadcasted_iota(jnp.int32, (BLOCK, width), 1)
            own = jnp.where(u <= t, own, LOW)
            highest = jnp.maximum(
                jnp.max(prefix, axis=1, keepdims=True), jnp.max(own, axis=1, keepdims=True)
            )
            prefix = jnp.exp(prefix - highest)
            own = jnp.exp(own - highest)
            totals = jnp.sum(prefix, axis=1, keepdims=True) + jnp.sum(own, axis=1, keepdims=True)
            mixed = dot(prefix.astype(BF16), prefix_values) + dot(own.astype(BF16), sv_v[:width, :])
            attn_out[rows, head] = (mixed / totals).astype(BF16)
        return carry

    lax.fori_loop(0, QH, attend, 0)

    arrived(local_a, 2)
    arrived(total_a, 3)

    def pick_final(d, carry):
        r = sources[d]
        start = held_a[holders[ids[r]]].astype(F32)
        fade = total_a[r]
        fade = jnp.concatenate([fade, fade], axis=1)
        final_p[d] = (start * fade + local_a[r].astype(F32)).astype(BF16)
        return carry

    lax.fori_loop(0, SLOTS, pick_final, 0)

    def store_final(k, carry):
        p = lax.rem(me + k, SLOTS)
        to_member(p, final_p.at[p], stored.at[0, me], 6).start()
        return carry

    lax.fori_loop(1, SLOTS, store_final, 0)
    own_final = pltpu.make_async_copy(final_p.at[me], stored.at[0, me], own_sem.at[2])
    own_final.start()

    loads[6].wait()
    arrived(held_b, 5)

    def gate_values(j, squares):
        pair = pl.ds(pl.multiple_of(j * 128, 128), 128)
        start = held_b[pl.ds(2 * j, 2)].reshape(2 * MDIM, STATE)
        values = y_v[j] + decay_v[j] * dot_nt(read_v[...], start)
        gate = gate_v[:, pair].astype(F32)
        values = values * (gate / (1.0 + jnp.exp(-gate)))
        y_v[j] = values
        return squares + values * values

    squares = lax.fori_loop(0, PAIRS, gate_values, jnp.zeros((ROWS, 128), F32))
    square_mine[...] = jnp.sum(jnp.transpose(squares), axis=0, keepdims=True)

    def send_squares(k, carry):
        pltpu.make_async_remote_copy(
            src_ref=square_mine,
            dst_ref=square_a.at[rank],
            send_sem=send_sem.at[7],
            recv_sem=recv_sem.at[7],
            device_id={"tensor": lax.rem(rank + k, RANKS)},
            device_id_type=MESH,
        ).start()
        return carry

    lax.fori_loop(1, RANKS, send_squares, 0)
    square_a[rank] = square_mine[...]
    arrived(square_a, 7, RANKS - 1)
    mean_square = jnp.sum(square_a[...], axis=0) / (MHEADS * MDIM)
    inverse = lax.rsqrt(mean_square + EPSILON)
    inverse = jnp.transpose(jnp.broadcast_to(inverse, (128, ROWS)))

    def norm(j, carry):
        pair = pl.ds(pl.multiple_of(j * 128, 128), 128)
        ssm_out[:, pair] = (y_v[j] * inverse * gain[pl.ds(j, 1), :]).astype(BF16)
        return carry

    lax.fori_loop(0, PAIRS, norm, 0)

    own_final.wait()
    sent(cache_a, 0)
    sent(held_a, 1)
    sent(local_a, 2)
    sent(total_a, 3)
    sent(cache_b, 4)
    sent(held_b, 5)
    sent(final_p, 6)
    sent(square_a, 7, RANKS - 1)
    part = stored.at[0, pl.ds(0, SLOTS - 1)]
    pltpu.make_async_copy(part, part, recv_sem.at[6]).wait()


def local(
    ssm_input,
    gate_input,
    step_sizes,
    decay_rates,
    state_write,
    state_read,
    norm_gain,
    queries,
    suffix_keys,
    suffix_values,
    held_state,
    held_cache,
    prefix_ids,
    prefix_lengths,
    holder_slots,
    new_holders,
):
    hbm = pl.BlockSpec(memory_space=pltpu.HBM)
    state = (SLOTS, MDIM, STATE)
    cache = (SLOTS, 2, PIECE, HDIM)
    outs = pl.pallas_call(
        kernel,
        out_shape=(
            pltpu.VMEM((ROWS, HEADS * MDIM), BF16),
            pltpu.VMEM((ROWS, QH * HDIM), BF16),
            pltpu.VMEM((1,) + state, BF16),
        ),
        in_specs=[hbm] * 16,
        out_specs=(pl.BlockSpec(memory_space=pltpu.VMEM),) * 3,
        scratch_shapes=[
            pltpu.SMEM((SLOTS,), jnp.int32),
            pltpu.SMEM((SLOTS,), jnp.int32),
            pltpu.SMEM((SLOTS,), jnp.int32),
            pltpu.SMEM((SLOTS,), jnp.int32),
            pltpu.SMEM((SLOTS,), jnp.int32),
            pltpu.SMEM((HEADS,), F32),
            pltpu.VMEM((HEADS, ROWS), F32),
            pltpu.VMEM((PAIRS, 128), F32),
            pltpu.VMEM((ROWS, HEADS * MDIM), BF16),
            pltpu.VMEM((ROWS, HEADS * MDIM), BF16),
            pltpu.VMEM((ROWS, STATE), BF16),
            pltpu.VMEM((ROWS, STATE), BF16),
            pltpu.VMEM((ROWS, QH * HDIM), BF16),
            pltpu.VMEM((ROWS, HDIM), BF16),
            pltpu.VMEM((ROWS, HDIM), BF16),
            pltpu.VMEM((HEADS, ROWS), F32),
            pltpu.VMEM((HEADS, ROWS), F32),
            pltpu.VMEM((HEADS, STATE), F32),
            pltpu.VMEM((2, BLOCK, BLOCK), F32),
            pltpu.VMEM((PAIRS, 2 * MDIM, STATE), BF16),
            pltpu.VMEM((PAIRS, ROWS, 128), F32),
            pltpu.VMEM((PAIRS, ROWS, 128), F32),
            pltpu.VMEM(state, BF16),
            pltpu.VMEM(cache, BF16),
            pltpu.VMEM(state, BF16),
            pltpu.VMEM(state, BF16),
            pltpu.VMEM((HEADS, 1, 128), F32),
            pltpu.VMEM((SLOTS, 1, 128), F32),
            pltpu.VMEM(state, BF16),
            pltpu.VMEM(state, BF16),
            pltpu.VMEM(cache, BF16),
            pltpu.VMEM(cache, BF16),
            pltpu.VMEM(state, BF16),
            pltpu.VMEM((1, ROWS), F32),
            pltpu.VMEM((RANKS, 1, ROWS), F32),
            pltpu.SemaphoreType.DMA((14,)),
            pltpu.SemaphoreType.DMA((3,)),
            pltpu.SemaphoreType.DMA((8,)),
            pltpu.SemaphoreType.DMA((8,)),
        ],
        compiler_params=pltpu.CompilerParams(
            collective_id=0, has_side_effects=True, vmem_limit_bytes=44 * 2**20
        ),
        name="layer_pair",
    )(*(pltpu.with_memory_space_constraint(a, pltpu.HBM) for a in (
        prefix_ids,
        prefix_lengths,
        holder_slots,
        new_holders,
        decay_rates,
        step_sizes,
        norm_gain.reshape(PAIRS, 128),
        ssm_input,
        gate_input,
        state_write,
        state_read,
        queries,
        suffix_keys,
        suffix_values,
        held_state,
        held_cache,
    )))
    return pl.pallas_call(
        hand_over,
        out_shape=tuple(jax.ShapeDtypeStruct(out.shape, out.dtype) for out in outs),
        in_specs=[pl.BlockSpec(memory_space=pltpu.VMEM)] * 3,
        out_specs=(hbm,) * 3,
        scratch_shapes=[pltpu.SemaphoreType.DMA((8,))],
        compiler_params=pltpu.CompilerParams(vmem_limit_bytes=2**20),
        name="hand_over",
    )(*outs)


def hand_over(ssm, attn, state, ssm_out, attn_out, stored, sem):
    copies = []
    for n in range(4):
        rows = pl.ds(n * 128, 128)
        copies.append((ssm.at[rows], ssm_out.at[rows]))
    for n in range(2):
        rows = pl.ds(n * 256, 256)
        copies.append((attn.at[rows], attn_out.at[rows]))
    for n in range(2):
        heads = pl.ds(n * 16, 16)
        copies.append((state.at[0, heads], stored.at[0, heads]))
    copies = [pltpu.make_async_copy(a, b, sem.at[n]) for n, (a, b) in enumerate(copies)]
    for c in copies:
        c.start()
    for c in copies:
        c.wait()


def solution(mesh):
    return jax.shard_map(
        local,
        mesh=mesh,
        in_specs=(
            P("group", "tensor"),
            P("group", "tensor"),
            P("tensor", "group"),
            P("tensor"),
            P("group", "tensor"),
            P("group", "tensor"),
            P("tensor"),
            P("group", "tensor"),
            P("group", "tensor"),
            P("group", "tensor"),
            P("group", "tensor", None, None),
            P("group", None, None, "tensor"),
            P(),
            P(),
            P(),
            P(),
        ),
        out_specs=(P("group", "tensor"), P("group", "tensor"), P("group", "tensor", None, None)),
        check_vma=False,
    )
```

```python
import jax
import jax.numpy as jnp
from jax import lax
from jax.experimental import pallas as pl
from jax.experimental.pallas import tpu as pltpu
from jax.sharding import PartitionSpec as P

MHEADS = 256
MDIM = 64
STATE = 256
HDIM = 128
BLOCK = 256
ROWS = 512
LP = 512
SLOTS = 32
HEADS = 32
PAIRS = HEADS // 2
QH = 8
RANKS = 8
PIECE = LP // SLOTS
EPSILON = 1e-05
LOW = -1e30
MESH = pl.DeviceIdType.MESH
F32 = jnp.float32
BF16 = jnp.bfloat16


def dot(a, b):
    return jnp.dot(a, b, preferred_element_type=F32)


def dot_nt(a, b):
    return lax.dot_general(a, b, (((1,), (1,)), ((), ())), preferred_element_type=F32)


def kernel(
    ids_hbm,
    lengths_hbm,
    holders_hbm,
    new_hbm,
    rates_hbm,
    steps_hbm,
    gain_hbm,
    x_hbm,
    gate_hbm,
    write_hbm,
    read_hbm,
    q_hbm,
    sk_hbm,
    sv_hbm,
    held,
    cache,
    ssm_out,
    attn_out,
    stored,
    ids,
    lengths,
    holders,
    new_holders,
    sources,
    rates,
    steps,
    gain,
    x_v,
    gate_v,
    write_v,
    read_v,
    q_v,
    sk_v,
    sv_v,
    cum_v,
    scale_v,
    fade_v,
    gram_v,
    entry_v,
    y_v,
    decay_v,
    held_a,
    cache_a,
    local_mine,
    local_a,
    total_mine,
    total_a,
    held_p,
    held_b,
    cache_p,
    cache_b,
    final_p,
    square_mine,
    square_a,
    in_sem,
    own_sem,
    send_sem,
    recv_sem,
):
    me = lax.axis_index("group")
    rank = lax.axis_index("tensor")

    barrier = pltpu.get_barrier_semaphore()

    def greet_member(k, carry):
        pl.semaphore_signal(
            barrier, inc=1, device_id={"group": lax.rem(me + k, SLOTS)}, device_id_type=MESH
        )
        return carry

    def greet_rank(k, carry):
        pl.semaphore_signal(
            barrier, inc=1, device_id={"tensor": lax.rem(rank + k, RANKS)}, device_id_type=MESH
        )
        return carry

    lax.fori_loop(1, SLOTS, greet_member, 0)
    lax.fori_loop(1, RANKS, greet_rank, 0)

    loads = []
    for n, (src, dst) in enumerate(
        (
            (x_hbm, x_v),
            (write_hbm, write_v),
            (read_hbm, read_v),
            (q_hbm, q_v),
            (sk_hbm, sk_v),
            (sv_hbm, sv_v),
            (gate_hbm, gate_v),
            (rates_hbm, rates),
            (steps_hbm, steps),
            (ids_hbm, ids),
            (lengths_hbm, lengths),
            (holders_hbm, holders),
            (new_hbm, new_holders),
            (gain_hbm, gain),
        )
    ):
        loads.append(pltpu.make_async_copy(src, dst, in_sem.at[n]))
        loads[-1].start()

    pl.semaphore_wait(barrier, SLOTS - 1 + RANKS - 1)

    def to_member(p, src, dst, n):
        return pltpu.make_async_remote_copy(
            src_ref=src,
            dst_ref=dst,
            send_sem=send_sem.at[n],
            recv_sem=recv_sem.at[n],
            device_id={"group": p},
            device_id_type=MESH,
        )

    def arrived(buf, n, count=SLOTS - 1):
        part = buf.at[pl.ds(0, count)]
        pltpu.make_async_copy(part, part, recv_sem.at[n]).wait()

    def sent(buf, n, count=SLOTS - 1):
        part = buf.at[pl.ds(0, count)]
        pltpu.make_async_copy(part, part, send_sem.at[n]).wait()

    turn = lax.rem(me, 2) + 2 * (me // 16)

    def in_order(zs, send):
        for z in zs:
            def one(k, carry, z=z):
                at = lax.rem(k + turn, 4)
                p = lax.rem(at, 2) + 2 * z + 16 * (at // 2)

                @pl.when(p != me)
                def _():
                    send(p)

                return carry

            lax.fori_loop(0, 4, one, 0)

    def cache_rows(p):
        return cache.at[0, :, pl.ds(pl.multiple_of(p * PIECE, PIECE), PIECE), :]

    def spread_cache(k, carry):
        p = lax.rem(me + k, SLOTS)
        to_member(p, cache_rows(p), cache_a.at[me], 0).start()
        return carry

    def spread_held(k, carry):
        p = lax.rem(me + k, SLOTS)
        to_member(p, held.at[0, p], held_a.at[me], 1).start()
        return carry

    lax.fori_loop(1, SLOTS, spread_cache, 0)
    lax.fori_loop(1, SLOTS, spread_held, 0)
    own_cache = pltpu.make_async_copy(cache_rows(me), cache_a.at[me], own_sem.at[0])
    own_held = pltpu.make_async_copy(held.at[0, me], held_a.at[me], own_sem.at[1])
    own_cache.start()
    own_held.start()

    loads[7].wait()
    loads[8].wait()

    def head_logs(h, carry):
        row = pl.ds(h, 1)
        cum_v[row, :] = steps[row, :] * -rates[h]
        return carry

    lax.fori_loop(0, HEADS, head_logs, 0)
    at_u = lax.broadcasted_iota(jnp.int32, (BLOCK, BLOCK), 0)
    at_t = lax.broadcasted_iota(jnp.int32, (BLOCK, BLOCK), 1)
    upper = (at_u <= at_t).astype(F32)
    ends = []
    for b in range(2):
        cols = slice(b * BLOCK, (b + 1) * BLOCK)
        cum = jnp.dot(
            cum_v[:, cols], upper, preferred_element_type=F32, precision=lax.Precision.HIGHEST
        )
        end = cum[:, BLOCK - 1 : BLOCK]
        cum_v[:, cols] = cum
        scale_v[:, cols] = jnp.exp(end - cum) * steps[:, cols]
        ends.append(end)
    fade_v[...] = jnp.broadcast_to(jnp.exp(ends[1]), (HEADS, STATE))
    total_mine[...] = jnp.broadcast_to(jnp.exp(ends[0] + ends[1]), (HEADS, 128)).reshape(
        HEADS, 1, 128
    )

    for n in range(9, 14):
        loads[n].wait()

    def find_source(d, carry):
        source = 0
        for r in range(1, SLOTS):
            source = jnp.where(new_holders[r] == d, r, source)
        sources[d] = source
        return carry

    lax.fori_loop(0, SLOTS, find_source, 0)

    loads[0].wait()
    loads[1].wait()
    first_row = lax.broadcasted_iota(jnp.int32, (2 * MDIM, 1), 0) < MDIM

    def local_state(j, carry):
        a, b = pl.ds(2 * j, 1), pl.ds(2 * j + 1, 1)
        pair = pl.ds(pl.multiple_of(j * 128, 128), 128)
        turned = jnp.transpose(x_v[:, pair].astype(F32))
        scaled = turned * jnp.where(first_row, scale_v[a, :], scale_v[b, :])
        high = scaled.astype(BF16)
        low = (scaled - high.astype(F32)).astype(BF16)
        early, late = write_v[:BLOCK, :], write_v[BLOCK:, :]
        entry = dot(high[:, :BLOCK], early) + dot(low[:, :BLOCK], early)
        later = dot(high[:, BLOCK:], late) + dot(low[:, BLOCK:], late)
        entry_v[j] = entry.astype(BF16)
        fade = jnp.where(first_row, fade_v[a, :], fade_v[b, :])
        local_mine[pl.ds(2 * j, 2)] = (
            (fade * entry + later).astype(BF16).reshape(2, MDIM, STATE)
        )
        return carry

    lax.fori_loop(0, PAIRS, local_state, 0)

    def spread_local(k, carry):
        p = lax.rem(me + k, SLOTS)
        to_member(p, local_mine.at[p], local_a.at[me], 2).start()
        to_member(p, total_mine.at[p], total_a.at[me], 3).start()
        return carry

    lax.fori_loop(1, SLOTS, spread_local, 0)
    local_a[me] = local_mine[me]
    total_a[me] = total_mine[me]

    own_cache.wait()
    arrived(cache_a, 0)

    def pick_cache(r, carry):
        cache_p[r] = cache_a[holders[ids[r]]]
        return carry

    lax.fori_loop(0, SLOTS, pick_cache, 0)

    def gather_cache(k, carry):
        p = lax.rem(me + k, SLOTS)
        to_member(p, cache_p.at[p], cache_b.at[me], 4).start()
        return carry

    lax.fori_loop(1, SLOTS, gather_cache, 0)
    cache_b[me] = cache_p[me]

    loads[2].wait()
    for b in range(2):
        rows = slice(b * BLOCK, (b + 1) * BLOCK)
        gram_v[b] = dot_nt(read_v[rows, :], write_v[rows, :])
    first_lane = lax.broadcasted_iota(jnp.int32, (1, 128), 1) < MDIM
    causal = at_u >= at_t

    def inner_values(j, carry):
        pair = pl.ds(pl.multiple_of(j * 128, 128), 128)
        xs = x_v[:, pair]
        zero = jnp.zeros_like(xs)
        halves = (jnp.where(first_lane, xs, zero), jnp.where(first_lane, zero, xs))
        tall = []
        values = [None, None]
        for i in range(2):
            row = pl.ds(2 * j + i, 1)
            cum = cum_v[row, :]
            column = jnp.transpose(jnp.broadcast_to(cum, (128, ROWS)))
            tall.append(column)
            for b in range(2):
                rows = slice(b * BLOCK, (b + 1) * BLOCK)
                left = column[rows, :]
                gap = jnp.concatenate([left, left], axis=1) - cum[:, rows]
                decays = jnp.exp(jnp.where(causal, gap, LOW))
                weights = (gram_v[b] * decays * steps[row, rows]).astype(BF16)
                part = dot(weights, halves[i][rows, :])
                values[b] = part if values[b] is None else values[b] + part
        column = jnp.where(first_lane, tall[0], tall[1])
        early, late = column[:BLOCK, :], column[BLOCK:, :]
        entered = dot_nt(read_v[BLOCK:, :], entry_v[j])
        decay_v[j, :BLOCK, :] = jnp.exp(early)
        decay_v[j, BLOCK:, :] = jnp.exp(late + early[BLOCK - 1 : BLOCK, :])
        y_v[j, :BLOCK, :] = values[0]
        y_v[j, BLOCK:, :] = values[1] + jnp.exp(late) * entered
        return carry

    lax.fori_loop(0, PAIRS, inner_values, 0)

    own_held.wait()
    arrived(held_a, 1)

    def pick_held(r, carry):
        held_p[r] = held_a[holders[ids[r]]]
        return carry

    lax.fori_loop(0, SLOTS, pick_held, 0)

    def gather_held(k, carry):
        p = lax.rem(me + k, SLOTS)
        to_member(p, held_p.at[p], held_b.at[me], 5).start()
        return carry

    lax.fori_loop(1, SLOTS, gather_held, 0)
    held_b[me] = held_p[me]

    for n in (3, 4, 5):
        loads[n].wait()
    arrived(cache_b, 4)
    length = lengths[ids[me]]
    prefix_allowed = lax.broadcasted_iota(jnp.int32, (1, LP), 1) < length
    score_scale = HDIM ** (-0.5)

    def attend(h, carry):
        head = pl.ds(pl.multiple_of(h * HDIM, HDIM), HDIM)
        prefix_keys = cache_b[:, 0].reshape(LP, HDIM)
        prefix_values = cache_b[:, 1].reshape(LP, HDIM)
        for b in range(2):
            rows = slice(b * BLOCK, (b + 1) * BLOCK)
            width = (b + 1) * BLOCK
            q = q_v[rows, head]
            prefix = dot_nt(q, prefix_keys) * score_scale
            prefix = jnp.where(prefix_allowed, prefix, LOW)
            own = dot_nt(q, sk_v[:width, :]) * score_scale
            t = lax.broadcasted_iota(jnp.int32, (BLOCK, width), 0) + b * BLOCK
            u = lax.broadcasted_iota(jnp.int32, (BLOCK, width), 1)
            own = jnp.where(u <= t, own, LOW)
            highest = jnp.maximum(
                jnp.max(prefix, axis=1, keepdims=True), jnp.max(own, axis=1, keepdims=True)
            )
            prefix = jnp.exp(prefix - highest)
            own = jnp.exp(own - highest)
            totals = jnp.sum(prefix, axis=1, keepdims=True) + jnp.sum(own, axis=1, keepdims=True)
            mixed = dot(prefix.astype(BF16), prefix_values) + dot(own.astype(BF16), sv_v[:width, :])
            attn_out[rows, head] = (mixed / totals).astype(BF16)
        return carry

    lax.fori_loop(0, QH, attend, 0)

    arrived(local_a, 2)
    arrived(total_a, 3)

    def pick_final(d, carry):
        r = sources[d]
        start = held_a[holders[ids[r]]].astype(F32)
        fade = total_a[r]
        fade = jnp.concatenate([fade, fade], axis=1)
        final_p[d] = (start * fade + local_a[r].astype(F32)).astype(BF16)
        return carry

    lax.fori_loop(0, SLOTS, pick_final, 0)

    in_order((0, 1, 2, 3, 7, 4, 6, 5), lambda p: to_member(p, final_p.at[p], stored.at[0, me], 6).start())
    own_final = pltpu.make_async_copy(final_p.at[me], stored.at[0, me], own_sem.at[2])
    own_final.start()

    loads[6].wait()
    arrived(held_b, 5)

    def gate_values(j, squares):
        pair = pl.ds(pl.multiple_of(j * 128, 128), 128)
        start = held_b[pl.ds(2 * j, 2)].reshape(2 * MDIM, STATE)
        values = y_v[j] + decay_v[j] * dot_nt(read_v[...], start)
        gate = gate_v[:, pair].astype(F32)
        values = values * (gate / (1.0 + jnp.exp(-gate)))
        y_v[j] = values
        return squares + values * values

    squares = lax.fori_loop(0, PAIRS, gate_values, jnp.zeros((ROWS, 128), F32))
    square_mine[...] = jnp.sum(jnp.transpose(squares), axis=0, keepdims=True)

    def send_squares(k, carry):
        pltpu.make_async_remote_copy(
            src_ref=square_mine,
            dst_ref=square_a.at[rank],
            send_sem=send_sem.at[7],
            recv_sem=recv_sem.at[7],
            device_id={"tensor": lax.rem(rank + k, RANKS)},
            device_id_type=MESH,
        ).start()
        return carry

    lax.fori_loop(1, RANKS, send_squares, 0)
    square_a[rank] = square_mine[...]
    arrived(square_a, 7, RANKS - 1)
    mean_square = jnp.sum(square_a[...], axis=0) / (MHEADS * MDIM)
    inverse = lax.rsqrt(mean_square + EPSILON)
    inverse = jnp.transpose(jnp.broadcast_to(inverse, (128, ROWS)))

    def norm(j, carry):
        pair = pl.ds(pl.multiple_of(j * 128, 128), 128)
        ssm_out[:, pair] = (y_v[j] * inverse * gain[pl.ds(j, 1), :]).astype(BF16)
        return carry

    lax.fori_loop(0, PAIRS, norm, 0)

    own_final.wait()
    sent(cache_a, 0)
    sent(held_a, 1)
    sent(local_a, 2)
    sent(total_a, 3)
    sent(cache_b, 4)
    sent(held_b, 5)
    sent(final_p, 6)
    sent(square_a, 7, RANKS - 1)
    part = stored.at[0, pl.ds(0, SLOTS - 1)]
    pltpu.make_async_copy(part, part, recv_sem.at[6]).wait()


def local(
    ssm_input,
    gate_input,
    step_sizes,
    decay_rates,
    state_write,
    state_read,
    norm_gain,
    queries,
    suffix_keys,
    suffix_values,
    held_state,
    held_cache,
    prefix_ids,
    prefix_lengths,
    holder_slots,
    new_holders,
):
    hbm = pl.BlockSpec(memory_space=pltpu.HBM)
    state = (SLOTS, MDIM, STATE)
    cache = (SLOTS, 2, PIECE, HDIM)
    outs = pl.pallas_call(
        kernel,
        out_shape=(
            pltpu.VMEM((ROWS, HEADS * MDIM), BF16),
            pltpu.VMEM((ROWS, QH * HDIM), BF16),
            pltpu.VMEM((1,) + state, BF16),
        ),
        in_specs=[hbm] * 16,
        out_specs=(pl.BlockSpec(memory_space=pltpu.VMEM),) * 3,
        scratch_shapes=[
            pltpu.SMEM((SLOTS,), jnp.int32),
            pltpu.SMEM((SLOTS,), jnp.int32),
            pltpu.SMEM((SLOTS,), jnp.int32),
            pltpu.SMEM((SLOTS,), jnp.int32),
            pltpu.SMEM((SLOTS,), jnp.int32),
            pltpu.SMEM((HEADS,), F32),
            pltpu.VMEM((HEADS, ROWS), F32),
            pltpu.VMEM((PAIRS, 128), F32),
            pltpu.VMEM((ROWS, HEADS * MDIM), BF16),
            pltpu.VMEM((ROWS, HEADS * MDIM), BF16),
            pltpu.VMEM((ROWS, STATE), BF16),
            pltpu.VMEM((ROWS, STATE), BF16),
            pltpu.VMEM((ROWS, QH * HDIM), BF16),
            pltpu.VMEM((ROWS, HDIM), BF16),
            pltpu.VMEM((ROWS, HDIM), BF16),
            pltpu.VMEM((HEADS, ROWS), F32),
            pltpu.VMEM((HEADS, ROWS), F32),
            pltpu.VMEM((HEADS, STATE), F32),
            pltpu.VMEM((2, BLOCK, BLOCK), F32),
            pltpu.VMEM((PAIRS, 2 * MDIM, STATE), BF16),
            pltpu.VMEM((PAIRS, ROWS, 128), F32),
            pltpu.VMEM((PAIRS, ROWS, 128), F32),
            pltpu.VMEM(state, BF16),
            pltpu.VMEM(cache, BF16),
            pltpu.VMEM(state, BF16),
            pltpu.VMEM(state, BF16),
            pltpu.VMEM((HEADS, 1, 128), F32),
            pltpu.VMEM((SLOTS, 1, 128), F32),
            pltpu.VMEM(state, BF16),
            pltpu.VMEM(state, BF16),
            pltpu.VMEM(cache, BF16),
            pltpu.VMEM(cache, BF16),
            pltpu.VMEM(state, BF16),
            pltpu.VMEM((1, ROWS), F32),
            pltpu.VMEM((RANKS, 1, ROWS), F32),
            pltpu.SemaphoreType.DMA((14,)),
            pltpu.SemaphoreType.DMA((3,)),
            pltpu.SemaphoreType.DMA((8,)),
            pltpu.SemaphoreType.DMA((8,)),
        ],
        compiler_params=pltpu.CompilerParams(
            collective_id=0, has_side_effects=True, vmem_limit_bytes=44 * 2**20
        ),
        name="layer_pair",
    )(*(pltpu.with_memory_space_constraint(a, pltpu.HBM) for a in (
        prefix_ids,
        prefix_lengths,
        holder_slots,
        new_holders,
        decay_rates,
        step_sizes,
        norm_gain.reshape(PAIRS, 128),
        ssm_input,
        gate_input,
        state_write,
        state_read,
        queries,
        suffix_keys,
        suffix_values,
        held_state,
        held_cache,
    )))
    return pl.pallas_call(
        hand_over,
        out_shape=tuple(jax.ShapeDtypeStruct(out.shape, out.dtype) for out in outs),
        in_specs=[pl.BlockSpec(memory_space=pltpu.VMEM)] * 3,
        out_specs=(hbm,) * 3,
        scratch_shapes=[pltpu.SemaphoreType.DMA((8,))],
        compiler_params=pltpu.CompilerParams(vmem_limit_bytes=2**20),
        name="hand_over",
    )(*outs)


def hand_over(ssm, attn, state, ssm_out, attn_out, stored, sem):
    copies = []
    for n in range(4):
        rows = pl.ds(n * 128, 128)
        copies.append((ssm.at[rows], ssm_out.at[rows]))
    for n in range(2):
        rows = pl.ds(n * 256, 256)
        copies.append((attn.at[rows], attn_out.at[rows]))
    for n in range(2):
        heads = pl.ds(n * 16, 16)
        copies.append((state.at[0, heads], stored.at[0, heads]))
    copies = [pltpu.make_async_copy(a, b, sem.at[n]) for n, (a, b) in enumerate(copies)]
    for c in copies:
        c.start()
    for c in copies:
        c.wait()


def solution(mesh):
    return jax.shard_map(
        local,
        mesh=mesh,
        in_specs=(
            P("group", "tensor"),
            P("group", "tensor"),
            P("tensor", "group"),
            P("tensor"),
            P("group", "tensor"),
            P("group", "tensor"),
            P("tensor"),
            P("group", "tensor"),
            P("group", "tensor"),
            P("group", "tensor"),
            P("group", "tensor", None, None),
            P("group", None, None, "tensor"),
            P(),
            P(),
            P(),
            P(),
        ),
        out_specs=(P("group", "tensor"), P("group", "tensor"), P("group", "tensor", None, None)),
        check_vma=False,
    )
```

```python
import jax
import jax.numpy as jnp
from jax import lax
from jax.experimental import pallas as pl
from jax.experimental.pallas import tpu as pltpu
from jax.sharding import PartitionSpec as P

MHEADS = 256
MDIM = 64
STATE = 256
HDIM = 128
BLOCK = 256
ROWS = 512
LP = 512
SLOTS = 32
HEADS = 32
PAIRS = HEADS // 2
QH = 8
RANKS = 8
PIECE = LP // SLOTS
EPSILON = 1e-05
LOW = -1e30
MESH = pl.DeviceIdType.MESH
F32 = jnp.float32
BF16 = jnp.bfloat16


def dot(a, b):
    return jnp.dot(a, b, preferred_element_type=F32)


def dot_nt(a, b):
    return lax.dot_general(a, b, (((1,), (1,)), ((), ())), preferred_element_type=F32)


def kernel(
    ids_hbm,
    lengths_hbm,
    holders_hbm,
    new_hbm,
    rates_hbm,
    steps_hbm,
    gain_hbm,
    x_hbm,
    gate_hbm,
    write_hbm,
    read_hbm,
    q_hbm,
    sk_hbm,
    sv_hbm,
    held,
    cache,
    ssm_out,
    attn_out,
    stored,
    ids,
    lengths,
    holders,
    new_holders,
    sources,
    rates,
    steps,
    gain,
    x_v,
    gate_v,
    write_v,
    read_v,
    q_v,
    sk_v,
    sv_v,
    cum_v,
    scale_v,
    fade_v,
    gram_v,
    entry_v,
    y_v,
    decay_v,
    held_a,
    cache_a,
    local_mine,
    local_a,
    total_mine,
    total_a,
    held_p,
    held_b,
    cache_p,
    cache_b,
    final_p,
    square_mine,
    square_a,
    in_sem,
    own_sem,
    send_sem,
    recv_sem,
):
    me = lax.axis_index("group")
    rank = lax.axis_index("tensor")

    barrier = pltpu.get_barrier_semaphore()

    def greet_member(k, carry):
        pl.semaphore_signal(
            barrier, inc=1, device_id={"group": lax.rem(me + k, SLOTS)}, device_id_type=MESH
        )
        return carry

    def greet_rank(k, carry):
        pl.semaphore_signal(
            barrier, inc=1, device_id={"tensor": lax.rem(rank + k, RANKS)}, device_id_type=MESH
        )
        return carry

    lax.fori_loop(1, SLOTS, greet_member, 0)
    lax.fori_loop(1, RANKS, greet_rank, 0)

    loads = []
    for n, (src, dst) in enumerate(
        (
            (x_hbm, x_v),
            (write_hbm, write_v),
            (read_hbm, read_v),
            (q_hbm, q_v),
            (sk_hbm, sk_v),
            (sv_hbm, sv_v),
            (gate_hbm, gate_v),
            (rates_hbm, rates),
            (steps_hbm, steps),
            (ids_hbm, ids),
            (lengths_hbm, lengths),
            (holders_hbm, holders),
            (new_hbm, new_holders),
            (gain_hbm, gain),
        )
    ):
        loads.append(pltpu.make_async_copy(src, dst, in_sem.at[n]))
        loads[-1].start()

    pl.semaphore_wait(barrier, SLOTS - 1 + RANKS - 1)

    def to_member(p, src, dst, n):
        return pltpu.make_async_remote_copy(
            src_ref=src,
            dst_ref=dst,
            send_sem=send_sem.at[n],
            recv_sem=recv_sem.at[n],
            device_id={"group": p},
            device_id_type=MESH,
        )

    def arrived(buf, n, count=SLOTS - 1):
        part = buf.at[pl.ds(0, count)]
        pltpu.make_async_copy(part, part, recv_sem.at[n]).wait()

    def sent(buf, n, count=SLOTS - 1):
        part = buf.at[pl.ds(0, count)]
        pltpu.make_async_copy(part, part, send_sem.at[n]).wait()

    turn = lax.rem(me, 2) + 2 * (me // 16)

    def in_order(zs, send):
        for z in zs:
            def one(k, carry, z=z):
                at = lax.rem(k + turn, 4)
                p = lax.rem(at, 2) + 2 * z + 16 * (at // 2)

                @pl.when(p != me)
                def _():
                    send(p)

                return carry

            lax.fori_loop(0, 4, one, 0)

    def cache_rows(p):
        return cache.at[0, :, pl.ds(pl.multiple_of(p * PIECE, PIECE), PIECE), :]

    def spread_cache(k, carry):
        p = lax.rem(me + k, SLOTS)
        to_member(p, cache_rows(p), cache_a.at[me], 0).start()
        return carry

    def spread_held(k, carry):
        p = lax.rem(me + k, SLOTS)
        to_member(p, held.at[0, p], held_a.at[me], 1).start()
        return carry

    lax.fori_loop(1, SLOTS, spread_cache, 0)
    lax.fori_loop(1, SLOTS, spread_held, 0)
    own_cache = pltpu.make_async_copy(cache_rows(me), cache_a.at[me], own_sem.at[0])
    own_held = pltpu.make_async_copy(held.at[0, me], held_a.at[me], own_sem.at[1])
    own_cache.start()
    own_held.start()

    loads[7].wait()
    loads[8].wait()

    def head_logs(h, carry):
        row = pl.ds(h, 1)
        cum_v[row, :] = steps[row, :] * -rates[h]
        return carry

    lax.fori_loop(0, HEADS, head_logs, 0)
    at_u = lax.broadcasted_iota(jnp.int32, (BLOCK, BLOCK), 0)
    at_t = lax.broadcasted_iota(jnp.int32, (BLOCK, BLOCK), 1)
    upper = (at_u <= at_t).astype(F32)
    ends = []
    for b in range(2):
        cols = slice(b * BLOCK, (b + 1) * BLOCK)
        cum = jnp.dot(
            cum_v[:, cols], upper, preferred_element_type=F32, precision=lax.Precision.HIGHEST
        )
        end = cum[:, BLOCK - 1 : BLOCK]
        cum_v[:, cols] = cum
        scale_v[:, cols] = jnp.exp(end - cum) * steps[:, cols]
        ends.append(end)
    fade_v[...] = jnp.broadcast_to(jnp.exp(ends[1]), (HEADS, STATE))
    total_mine[...] = jnp.broadcast_to(jnp.exp(ends[0] + ends[1]), (HEADS, 128)).reshape(
        HEADS, 1, 128
    )

    def spread_total(k, carry):
        p = lax.rem(me + k, SLOTS)
        to_member(p, total_mine.at[p], total_a.at[me], 3).start()
        return carry

    lax.fori_loop(1, SLOTS, spread_total, 0)
    total_a[me] = total_mine[me]

    for n in range(9, 14):
        loads[n].wait()

    def find_source(d, carry):
        source = 0
        for r in range(1, SLOTS):
            source = jnp.where(new_holders[r] == d, r, source)
        sources[d] = source
        return carry

    lax.fori_loop(0, SLOTS, find_source, 0)

    loads[0].wait()
    loads[1].wait()
    first_row = lax.broadcasted_iota(jnp.int32, (2 * MDIM, 1), 0) < MDIM

    def local_state(j, carry):
        a, b = pl.ds(2 * j, 1), pl.ds(2 * j + 1, 1)
        pair = pl.ds(pl.multiple_of(j * 128, 128), 128)
        turned = jnp.transpose(x_v[:, pair].astype(F32))
        scaled = turned * jnp.where(first_row, scale_v[a, :], scale_v[b, :])
        high = scaled.astype(BF16)
        low = (scaled - high.astype(F32)).astype(BF16)
        early, late = write_v[:BLOCK, :], write_v[BLOCK:, :]
        entry = dot(high[:, :BLOCK], early) + dot(low[:, :BLOCK], early)
        later = dot(high[:, BLOCK:], late) + dot(low[:, BLOCK:], late)
        entry_v[j] = entry.astype(BF16)
        fade = jnp.where(first_row, fade_v[a, :], fade_v[b, :])
        local_mine[pl.ds(2 * j, 2)] = (
            (fade * entry + later).astype(BF16).reshape(2, MDIM, STATE)
        )
        return carry

    lax.fori_loop(0, PAIRS, local_state, 0)

    def spread_local(k, carry):
        p = lax.rem(me + k, SLOTS)
        to_member(p, local_mine.at[p], local_a.at[me], 2).start()
        return carry

    lax.fori_loop(1, SLOTS, spread_local, 0)
    local_a[me] = local_mine[me]

    own_cache.wait()
    arrived(cache_a, 0)

    def pick_cache(r, carry):
        cache_p[r] = cache_a[holders[ids[r]]]
        return carry

    lax.fori_loop(0, SLOTS, pick_cache, 0)

    def gather_cache(k, carry):
        p = lax.rem(me + k, SLOTS)
        to_member(p, cache_p.at[p], cache_b.at[me], 4).start()
        return carry

    lax.fori_loop(1, SLOTS, gather_cache, 0)
    cache_b[me] = cache_p[me]

    loads[2].wait()
    for b in range(2):
        rows = slice(b * BLOCK, (b + 1) * BLOCK)
        gram_v[b] = dot_nt(read_v[rows, :], write_v[rows, :])
    first_lane = lax.broadcasted_iota(jnp.int32, (1, 128), 1) < MDIM
    causal = at_u >= at_t

    def inner_values(j, carry):
        pair = pl.ds(pl.multiple_of(j * 128, 128), 128)
        xs = x_v[:, pair]
        zero = jnp.zeros_like(xs)
        halves = (jnp.where(first_lane, xs, zero), jnp.where(first_lane, zero, xs))
        tall = []
        values = [None, None]
        for i in range(2):
            row = pl.ds(2 * j + i, 1)
            cum = cum_v[row, :]
            column = jnp.transpose(jnp.broadcast_to(cum, (128, ROWS)))
            tall.append(column)
            for b in range(2):
                rows = slice(b * BLOCK, (b + 1) * BLOCK)
                left = column[rows, :]
                gap = jnp.concatenate([left, left], axis=1) - cum[:, rows]
                decays = jnp.exp(jnp.where(causal, gap, LOW))
                weights = (gram_v[b] * decays * steps[row, rows]).astype(BF16)
                part = dot(weights, halves[i][rows, :])
                values[b] = part if values[b] is None else values[b] + part
        column = jnp.where(first_lane, tall[0], tall[1])
        early, late = column[:BLOCK, :], column[BLOCK:, :]
        entered = dot_nt(read_v[BLOCK:, :], entry_v[j])
        decay_v[j, :BLOCK, :] = jnp.exp(early)
        decay_v[j, BLOCK:, :] = jnp.exp(late + early[BLOCK - 1 : BLOCK, :])
        y_v[j, :BLOCK, :] = values[0]
        y_v[j, BLOCK:, :] = values[1] + jnp.exp(late) * entered
        return carry

    lax.fori_loop(0, PAIRS, inner_values, 0)

    own_held.wait()
    arrived(held_a, 1)

    def pick_held(r, carry):
        held_p[r] = held_a[holders[ids[r]]]
        return carry

    lax.fori_loop(0, SLOTS, pick_held, 0)

    def gather_held(k, carry):
        p = lax.rem(me + k, SLOTS)
        to_member(p, held_p.at[p], held_b.at[me], 5).start()
        return carry

    lax.fori_loop(1, SLOTS, gather_held, 0)
    held_b[me] = held_p[me]

    for n in (3, 4, 5):
        loads[n].wait()
    arrived(cache_b, 4)
    length = lengths[ids[me]]
    prefix_allowed = lax.broadcasted_iota(jnp.int32, (1, LP), 1) < length
    score_scale = HDIM ** (-0.5)

    def attend(h, carry):
        head = pl.ds(pl.multiple_of(h * HDIM, HDIM), HDIM)
        prefix_keys = cache_b[:, 0].reshape(LP, HDIM)
        prefix_values = cache_b[:, 1].reshape(LP, HDIM)
        for b in range(2):
            rows = slice(b * BLOCK, (b + 1) * BLOCK)
            width = (b + 1) * BLOCK
            q = q_v[rows, head]
            prefix = dot_nt(q, prefix_keys) * score_scale
            prefix = jnp.where(prefix_allowed, prefix, LOW)
            own = dot_nt(q, sk_v[:width, :]) * score_scale
            t = lax.broadcasted_iota(jnp.int32, (BLOCK, width), 0) + b * BLOCK
            u = lax.broadcasted_iota(jnp.int32, (BLOCK, width), 1)
            own = jnp.where(u <= t, own, LOW)
            highest = jnp.maximum(
                jnp.max(prefix, axis=1, keepdims=True), jnp.max(own, axis=1, keepdims=True)
            )
            prefix = jnp.exp(prefix - highest)
            own = jnp.exp(own - highest)
            totals = jnp.sum(prefix, axis=1, keepdims=True) + jnp.sum(own, axis=1, keepdims=True)
            mixed = dot(prefix.astype(BF16), prefix_values) + dot(own.astype(BF16), sv_v[:width, :])
            attn_out[rows, head] = (mixed / totals).astype(BF16)
        return carry

    lax.fori_loop(0, QH, attend, 0)

    arrived(local_a, 2)
    arrived(total_a, 3)

    def pick_final(d, carry):
        r = sources[d]
        start = held_a[holders[ids[r]]].astype(F32)
        fade = total_a[r]
        fade = jnp.concatenate([fade, fade], axis=1)
        final_p[d] = (start * fade + local_a[r].astype(F32)).astype(BF16)
        return carry

    lax.fori_loop(0, SLOTS, pick_final, 0)

    in_order((0,), lambda p: to_member(p, final_p.at[p], stored.at[0, me], 6).start())

    def store_final(k, carry):
        p = lax.rem(me + k, SLOTS)

        @pl.when(lax.rem(p // 2, 8) >= 1)
        def _():
            to_member(p, final_p.at[p], stored.at[0, me], 6).start()

        return carry

    lax.fori_loop(1, SLOTS, store_final, 0)
    own_final = pltpu.make_async_copy(final_p.at[me], stored.at[0, me], own_sem.at[2])
    own_final.start()

    loads[6].wait()
    arrived(held_b, 5)

    def gate_values(j, squares):
        pair = pl.ds(pl.multiple_of(j * 128, 128), 128)
        start = held_b[pl.ds(2 * j, 2)].reshape(2 * MDIM, STATE)
        values = y_v[j] + decay_v[j] * dot_nt(read_v[...], start)
        gate = gate_v[:, pair].astype(F32)
        values = values * (gate / (1.0 + jnp.exp(-gate)))
        y_v[j] = values
        return squares + values * values

    squares = lax.fori_loop(0, PAIRS, gate_values, jnp.zeros((ROWS, 128), F32))
    square_mine[...] = jnp.sum(jnp.transpose(squares), axis=0, keepdims=True)

    def send_squares(k, carry):
        pltpu.make_async_remote_copy(
            src_ref=square_mine,
            dst_ref=square_a.at[rank],
            send_sem=send_sem.at[7],
            recv_sem=recv_sem.at[7],
            device_id={"tensor": lax.rem(rank + k, RANKS)},
            device_id_type=MESH,
        ).start()
        return carry

    lax.fori_loop(1, RANKS, send_squares, 0)
    square_a[rank] = square_mine[...]
    arrived(square_a, 7, RANKS - 1)
    mean_square = jnp.sum(square_a[...], axis=0) / (MHEADS * MDIM)
    inverse = lax.rsqrt(mean_square + EPSILON)
    inverse = jnp.transpose(jnp.broadcast_to(inverse, (128, ROWS)))

    def norm(j, carry):
        pair = pl.ds(pl.multiple_of(j * 128, 128), 128)
        ssm_out[:, pair] = (y_v[j] * inverse * gain[pl.ds(j, 1), :]).astype(BF16)
        return carry

    lax.fori_loop(0, PAIRS, norm, 0)

    own_final.wait()
    sent(cache_a, 0)
    sent(held_a, 1)
    sent(local_a, 2)
    sent(total_a, 3)
    sent(cache_b, 4)
    sent(held_b, 5)
    sent(final_p, 6)
    sent(square_a, 7, RANKS - 1)
    part = stored.at[0, pl.ds(0, SLOTS - 1)]
    pltpu.make_async_copy(part, part, recv_sem.at[6]).wait()


def local(
    ssm_input,
    gate_input,
    step_sizes,
    decay_rates,
    state_write,
    state_read,
    norm_gain,
    queries,
    suffix_keys,
    suffix_values,
    held_state,
    held_cache,
    prefix_ids,
    prefix_lengths,
    holder_slots,
    new_holders,
):
    hbm = pl.BlockSpec(memory_space=pltpu.HBM)
    state = (SLOTS, MDIM, STATE)
    cache = (SLOTS, 2, PIECE, HDIM)
    outs = pl.pallas_call(
        kernel,
        out_shape=(
            pltpu.VMEM((ROWS, HEADS * MDIM), BF16),
            pltpu.VMEM((ROWS, QH * HDIM), BF16),
            pltpu.VMEM((1,) + state, BF16),
        ),
        in_specs=[hbm] * 16,
        out_specs=(pl.BlockSpec(memory_space=pltpu.VMEM),) * 3,
        scratch_shapes=[
            pltpu.SMEM((SLOTS,), jnp.int32),
            pltpu.SMEM((SLOTS,), jnp.int32),
            pltpu.SMEM((SLOTS,), jnp.int32),
            pltpu.SMEM((SLOTS,), jnp.int32),
            pltpu.SMEM((SLOTS,), jnp.int32),
            pltpu.SMEM((HEADS,), F32),
            pltpu.VMEM((HEADS, ROWS), F32),
            pltpu.VMEM((PAIRS, 128), F32),
            pltpu.VMEM((ROWS, HEADS * MDIM), BF16),
            pltpu.VMEM((ROWS, HEADS * MDIM), BF16),
            pltpu.VMEM((ROWS, STATE), BF16),
            pltpu.VMEM((ROWS, STATE), BF16),
            pltpu.VMEM((ROWS, QH * HDIM), BF16),
            pltpu.VMEM((ROWS, HDIM), BF16),
            pltpu.VMEM((ROWS, HDIM), BF16),
            pltpu.VMEM((HEADS, ROWS), F32),
            pltpu.VMEM((HEADS, ROWS), F32),
            pltpu.VMEM((HEADS, STATE), F32),
            pltpu.VMEM((2, BLOCK, BLOCK), F32),
            pltpu.VMEM((PAIRS, 2 * MDIM, STATE), BF16),
            pltpu.VMEM((PAIRS, ROWS, 128), F32),
            pltpu.VMEM((PAIRS, ROWS, 128), F32),
            pltpu.VMEM(state, BF16),
            pltpu.VMEM(cache, BF16),
            pltpu.VMEM(state, BF16),
            pltpu.VMEM(state, BF16),
            pltpu.VMEM((HEADS, 1, 128), F32),
            pltpu.VMEM((SLOTS, 1, 128), F32),
            pltpu.VMEM(state, BF16),
            pltpu.VMEM(state, BF16),
            pltpu.VMEM(cache, BF16),
            pltpu.VMEM(cache, BF16),
            pltpu.VMEM(state, BF16),
            pltpu.VMEM((1, ROWS), F32),
            pltpu.VMEM((RANKS, 1, ROWS), F32),
            pltpu.SemaphoreType.DMA((14,)),
            pltpu.SemaphoreType.DMA((3,)),
            pltpu.SemaphoreType.DMA((8,)),
            pltpu.SemaphoreType.DMA((8,)),
        ],
        compiler_params=pltpu.CompilerParams(
            collective_id=0, has_side_effects=True, vmem_limit_bytes=44 * 2**20
        ),
        name="layer_pair",
    )(*(pltpu.with_memory_space_constraint(a, pltpu.HBM) for a in (
        prefix_ids,
        prefix_lengths,
        holder_slots,
        new_holders,
        decay_rates,
        step_sizes,
        norm_gain.reshape(PAIRS, 128),
        ssm_input,
        gate_input,
        state_write,
        state_read,
        queries,
        suffix_keys,
        suffix_values,
        held_state,
        held_cache,
    )))
    return pl.pallas_call(
        hand_over,
        out_shape=tuple(jax.ShapeDtypeStruct(out.shape, out.dtype) for out in outs),
        in_specs=[pl.BlockSpec(memory_space=pltpu.VMEM)] * 3,
        out_specs=(hbm,) * 3,
        scratch_shapes=[pltpu.SemaphoreType.DMA((8,))],
        compiler_params=pltpu.CompilerParams(vmem_limit_bytes=2**20),
        name="hand_over",
    )(*outs)


def hand_over(ssm, attn, state, ssm_out, attn_out, stored, sem):
    copies = []
    for n in range(4):
        rows = pl.ds(n * 128, 128)
        copies.append((ssm.at[rows], ssm_out.at[rows]))
    for n in range(2):
        rows = pl.ds(n * 256, 256)
        copies.append((attn.at[rows], attn_out.at[rows]))
    for n in range(2):
        heads = pl.ds(n * 16, 16)
        copies.append((state.at[0, heads], stored.at[0, heads]))
    copies = [pltpu.make_async_copy(a, b, sem.at[n]) for n, (a, b) in enumerate(copies)]
    for c in copies:
        c.start()
    for c in copies:
        c.wait()


def solution(mesh):
    return jax.shard_map(
        local,
        mesh=mesh,
        in_specs=(
            P("group", "tensor"),
            P("group", "tensor"),
            P("tensor", "group"),
            P("tensor"),
            P("group", "tensor"),
            P("group", "tensor"),
            P("tensor"),
            P("group", "tensor"),
            P("group", "tensor"),
            P("group", "tensor"),
            P("group", "tensor", None, None),
            P("group", None, None, "tensor"),
            P(),
            P(),
            P(),
            P(),
        ),
        out_specs=(P("group", "tensor"), P("group", "tensor"), P("group", "tensor", None, None)),
        check_vma=False,
    )
```
